256 devices in a mesh: ctx: 32 (over z_hi, y, core), dp: 8 (over x, z_lo).
Axes of the slice: x: 4, y: 4, z: 8 (z_hi: 4, z_lo: 2; z = z_hi * 2 + z_lo), core: 2. Of those that a mesh axis runs over, the one named last changes fastest.
Arguments:
- query_rows: bfloat16 [49152, 1536], P(('dp', 'ctx')), parts along dimension 0, may hold values from -5 to 5
- key_rows: bfloat16 [49152, 512], P(('dp', 'ctx')), parts along dimension 0, may hold values from -5 to 5
- value_rows: bfloat16 [49152, 512], P(('dp', 'ctx')), parts along dimension 0, may hold values from -6 to 6
- out_grad: bfloat16 [49152, 1536], P(('dp', 'ctx')), parts along dimension 0, may hold values from -6 to 6
- token_span: int32 [49152], P('dp'), parts along dimension 0, may hold values from 0 to 15, never falling along the last dimension, each value on 1 to 768 neighbouring positions
- visible: int32 [128, 16], P('dp'), parts along dimension 0, may hold values from 0 to 1, as said below
Outputs:
- grad_query: bfloat16 [49152, 1536], P(('dp', 'ctx')), parts along dimension 0
- grad_key: bfloat16 [49152, 512], P(('dp', 'ctx')), parts along dimension 0
- grad_value: bfloat16 [49152, 512], P(('dp', 'ctx')), parts along dimension 0
The draws below stay inside these ranges and needn't reach their ends.
There are 8 independent parts, one for each index of `dp`. The reference program is written for one: setup_inputs(seed, part) draws one part's arguments, and reference() takes and returns one part's arrays. A program takes and returns all parts, laid end to end along the dimension named above; each array names one. Nothing has to cross between parts.
Inputs may be any that keep to these rules, and one draw needn't show every extreme that they name: visible[i][i] is 1 and visible[i][j] is 0 for j > i.
All inputs are finite; a program needn't handle non-finite values.
Results may differ from the reference program's by a relative error of at most 0.018.
Values may be sent and summed in bfloat16 or wider, within the bound.
No kernel may reach another device: no remote copies, remote signals or barrier semaphores. Data moves between devices by JAX's collectives and lax.ppermute only.
A program may use at most 128 MiB of HBM per device.

```python
import math
import jax
import jax.numpy as jnp
import numpy as np
from jax import lax

HEADS = 12
KV_HEADS = 4
HEAD = 128
TOK_DEV = 192
SPANS = 16
TOKENS = 6144
SPAN_MOST = 768


def draw_query_rows(key, part):
    key = jax.random.fold_in(key, 11)
    entries = jnp.clip(jax.random.normal(key, (TOKENS, HEADS * HEAD), jnp.float32), -4.5, 4.5)
    return entries.astype(jnp.bfloat16)


def draw_key_rows(key, part):
    key = jax.random.fold_in(key, 23)
    entries = jnp.clip(jax.random.normal(key, (TOKENS, KV_HEADS * HEAD), jnp.float32), -4.5, 4.5)
    return entries.astype(jnp.bfloat16)


def draw_visible(key, part):
    key = jax.random.fold_in(key, 5)
    coins = jax.random.randint(key, (SPANS, SPANS), 0, 4)
    row_ids = jnp.arange(SPANS)[:, None]
    col_ids = jnp.arange(SPANS)[None, :]
    earlier = jnp.logical_and(col_ids < row_ids, coins > 0)
    return jnp.where(jnp.logical_or(col_ids == row_ids, earlier), 1, 0).astype(jnp.int32)


def shard_levels(stream_key, extent, pieces, low, largest):
    factor_of = 1.0
    for position, shards_of in pieces:
        draws = jax.random.uniform(jax.random.fold_in(jax.random.fold_in(stream_key, 6), position), (shards_of,), jnp.float32, low / len(pieces), largest / len(pieces))
        factor_of = factor_of * jnp.repeat(jnp.exp(draws), extent[position] // shards_of).reshape((-1,) + (1,) * (len(extent) - 1 - position))
    return factor_of


def profile(amount, total, reach, skew):
    portions = [(1 << 20) // math.isqrt(rank ** skew) + 1 for rank in range(2, amount + 1)]
    surplus, given = total - reach - (amount - 1), [1] * (amount - 1)
    while surplus > 0:
        free = [i for i in range(amount - 1) if given[i] < reach]
        whole, left = sum([portions[i] for i in free]), surplus
        for i in free:
            more = min(reach - given[i], max(1, left * portions[i] // whole), surplus)
            given[i] = given[i] + more
            surplus = surplus - more
    return np.array([reach] + given)


def uneven(stream_key, amount, total, most, skew):
    if amount == 2:
        one = jax.random.randint(stream_key, (), max(1, total - most), min(most, total - 1) + 1)
        return jnp.stack([one, total - one])
    sizes = jnp.asarray(profile(amount, total, most, skew), jnp.int32)
    twos = (amount - 1) // 2
    giver, taker = sizes[1:1 + 2 * twos:2], sizes[2:2 + 2 * twos:2]
    room = jnp.minimum(giver - 1, most - taker)
    shifted = jax.random.randint(jax.random.fold_in(stream_key, 1), (twos,), 0, 1 << 20) % (room + 1)
    sizes = sizes.at[1:1 + 2 * twos:2].set(giver - shifted).at[2:2 + 2 * twos:2].set(taker + shifted)
    return sizes[jax.random.permutation(jax.random.fold_in(stream_key, 2), amount)]


def bell_draw(key, extent, width, reach, cuts=(), kind=jnp.bfloat16):
    level = shard_levels(key, extent, cuts, -0.22, 0.18) if cuts else 1.0
    values = jax.random.normal(key, extent, jnp.float32) * width * level
    return jnp.minimum(jnp.maximum(values, -reach), reach).astype(kind)


def setup_inputs(seed: int = 0, part: int = 0) -> dict:
    arg_keys = jax.random.split(jax.random.key(seed), 7)
    own_keys = jax.random.split(jax.random.fold_in(arg_keys[6], part), 7)
    return {
        "query_rows": draw_query_rows(jax.random.fold_in(jax.random.fold_in(arg_keys[6], part), 71), part),
        "key_rows": draw_key_rows(jax.random.fold_in(jax.random.fold_in(arg_keys[6], part), 71), part),
        "value_rows": bell_draw(own_keys[2], (TOKENS, KV_HEADS * HEAD), 1.0, 6.0, ((0, 32),)),
        "out_grad": bell_draw(own_keys[3], (TOKENS, HEADS * HEAD), 1.0, 6.0, ((0, 32),)),
        "token_span": jnp.searchsorted(jnp.cumsum(uneven(own_keys[4], SPANS, TOKENS, SPAN_MOST, 1)), jnp.arange(TOKENS), side="right").astype(jnp.int32),
        "visible": draw_visible(jax.random.fold_in(jax.random.fold_in(arg_keys[6], part), 71), part),
    }


def allowed_table(visible, row_spans, col_spans):
    return jnp.take(jnp.take(visible, row_spans, axis=0), col_spans, axis=1) > 0


def reference(query_rows, key_rows, value_rows, out_grad, token_span, visible):
    group_size = HEADS // KV_HEADS
    scaling = HEAD ** -0.5
    query_heads = query_rows.reshape(TOKENS, KV_HEADS, group_size, HEAD)
    grad_heads = out_grad.reshape(TOKENS, KV_HEADS, group_size, HEAD)
    key_full = key_rows.reshape(TOKENS, KV_HEADS, HEAD).astype(jnp.float32)
    value_full = value_rows.reshape(TOKENS, KV_HEADS, HEAD).astype(jnp.float32)
    block_count = TOKENS // TOK_DEV

    def query_step(state, block_index):
        dk_sum, dv_sum = state
        first_row = (block_index * TOK_DEV).astype(jnp.int32)
        query_block = lax.dynamic_slice_in_dim(query_heads, first_row, TOK_DEV, 0).astype(jnp.float32)
        grad_block = lax.dynamic_slice_in_dim(grad_heads, first_row, TOK_DEV, 0).astype(jnp.float32)
        span_block = lax.dynamic_slice_in_dim(token_span, first_row, TOK_DEV, 0)
        seen_mask = allowed_table(visible, span_block, token_span)[None, None]
        raw_scores = jnp.einsum("qcgd,kcd->cgqk", query_block, key_full) * scaling
        row_top = jnp.max(jnp.where(seen_mask, raw_scores, -1e30), axis=-1, keepdims=True)
        row_total = jnp.sum(jnp.where(seen_mask, jnp.exp(raw_scores - row_top), 0.0), axis=-1, keepdims=True)
        log_total = row_top + jnp.log(row_total)
        probs_full = jnp.where(seen_mask, jnp.exp(raw_scores - log_total), 0.0)
        probs_low = lax.optimization_barrier(probs_full.astype(jnp.bfloat16)).astype(jnp.float32)
        output = jnp.einsum("cgqk,kcd->qcgd", probs_low, value_full)
        row_delta = jnp.transpose(jnp.sum(grad_block * output, axis=-1), (1, 2, 0))
        dprobs = jnp.einsum("qcgd,kcd->cgqk", grad_block, value_full)
        dscores = probs_full * (dprobs - row_delta[..., None])
        dscores_low = lax.optimization_barrier(dscores.astype(jnp.bfloat16)).astype(jnp.float32)
        dq_block = jnp.einsum("cgqk,kcd->qcgd", dscores_low, key_full) * scaling
        dk_block = jnp.einsum("cgqk,qcgd->kcd", dscores_low, query_block) * scaling
        dv_block = jnp.einsum("cgqk,qcgd->kcd", probs_low, grad_block)
        dk_part = lax.optimization_barrier(dk_block.astype(jnp.bfloat16)).astype(jnp.float32)
        dv_part = lax.optimization_barrier(dv_block.astype(jnp.bfloat16)).astype(jnp.float32)
        return (dk_sum + dk_part, dv_sum + dv_part), dq_block.astype(jnp.bfloat16)

    zeros_kv = jnp.zeros((TOKENS, KV_HEADS, HEAD), jnp.float32)
    (dk_sum, dv_sum), dq_parts = lax.scan(query_step, (zeros_kv, zeros_kv), jnp.arange(block_count, dtype=jnp.int32))
    grad_query = dq_parts.reshape(TOKENS, HEADS * HEAD)
    grad_key = dk_sum.astype(jnp.bfloat16).reshape(TOKENS, KV_HEADS * HEAD)
    grad_value = dv_sum.astype(jnp.bfloat16).reshape(TOKENS, KV_HEADS * HEAD)
    return (grad_query, grad_key, grad_value)
```

```python
import functools

import jax
import jax.numpy as jnp
import numpy as np
from jax import lax
from jax.experimental import pallas as pl
from jax.experimental.pallas import tpu as pltpu
from jax.sharding import Mesh, PartitionSpec as P

HEADS = 12
KV_HEADS = 4
GROUP = HEADS // KV_HEADS
HEAD = 128
SCALE = HEAD ** -0.5
LOG2E = 1.4426950408889634
NEG = -1e30
Z, Y, C = 4, 4, 2
T = Y * C
BLK = 192
QT = 256
NQ = Z * BLK // QT
PAIR = 2
KT = PAIR * BLK
NK = Z * T // PAIR
F32 = jnp.float32
BF16 = jnp.bfloat16


def dot(a, b):
    return lax.dot_general(a, b, (((1,), (0,)), ((), ())), preferred_element_type=F32)


def dot_tn(a, b):
    return lax.dot_general(a, b, (((0,), (0,)), ((), ())), preferred_element_type=F32)


def fold(x, op):
    return op(x.reshape(x.shape[0] // 8, 8, x.shape[1]), axis=0)


def attn_kernel(flags, qd_ref, kv_ref, hot_ref, bias_ref, dq_ref, dkv_ref,
                acc, sbuf, pbuf, qt, dot_t, qs, dos, stat_m, stat_l, stat_d, dqt):
    r = pl.program_id(0)

    @pl.when(r == 0)
    def _():
        acc[...] = jnp.zeros_like(acc)

    for h in range(GROUP):
        q = qd_ref[:, h * HEAD:(h + 1) * HEAD]
        g = qd_ref[:, (GROUP + h) * HEAD:(GROUP + h + 1) * HEAD]
        qt[h, :HEAD, :] = q.T
        qt[h, HEAD:, :] = bias_ref[0]
        dot_t[h] = g.T
    stat_m[...] = jnp.full_like(stat_m, NEG)
    stat_l[...] = jnp.zeros_like(stat_l)
    stat_d[...] = jnp.zeros_like(stat_d)
    dqt[...] = jnp.zeros_like(dqt)

    def place(n):
        return n // (T // PAIR), (n % (T // PAIR)) * PAIR

    def rows_of(n, lo):
        zq, t = place(n)
        return jnp.concatenate([kv_ref[t + i, zq, :, lo:lo + HEAD] for i in range(PAIR)], axis=0)

    def over_tiles(body):
        def step(n, carry):
            @pl.when(flags[r * NK + n] > 0)
            def _():
                body(n)
            return carry
        lax.fori_loop(0, NK, step, 0)

    def scores(n):
        zq, t = place(n)
        hot = jnp.concatenate([hot_ref[t + i, zq] for i in range(PAIR)], axis=0)
        lhs = jnp.concatenate([rows_of(n, 0), hot], axis=1)
        for h in range(GROUP):
            s = dot(lhs, qt[h])
            sbuf[n, :, h * QT:(h + 1) * QT] = s
            stat_m[h] = jnp.maximum(stat_m[h], fold(s, jnp.max))

    over_tiles(scores)
    tops = [jnp.max(stat_m[h], axis=0, keepdims=True) for h in range(GROUP)]
    for h in range(GROUP):
        stat_m[h] = jnp.broadcast_to(tops[h], (8, QT))

    def weights(n):
        v = rows_of(n, HEAD)
        for h in range(GROUP):
            cols = slice(h * QT, (h + 1) * QT)
            p = jnp.exp2((sbuf[n, :, cols] - stat_m[h, :1]) * (SCALE * LOG2E))
            dp = dot(v, dot_t[h])
            stat_l[h] += fold(p, jnp.sum)
            stat_d[h] += fold(p * dp, jnp.sum)
            pbuf[n, :, cols] = p.astype(BF16)
            sbuf[n, :, cols] = dp

    over_tiles(weights)
    invs = []
    for h in range(GROUP):
        inv = 1.0 / jnp.sum(stat_l[h], axis=0, keepdims=True)
        delta = jnp.sum(stat_d[h], axis=0, keepdims=True) * inv
        stat_d[h] = jnp.broadcast_to(delta, (8, QT))
        col = jnp.broadcast_to(inv, (HEAD, QT)).T
        q = qd_ref[:, h * HEAD:(h + 1) * HEAD].astype(F32)
        g = qd_ref[:, (GROUP + h) * HEAD:(GROUP + h + 1) * HEAD].astype(F32)
        qs[h] = (q * (col * SCALE)).astype(BF16)
        dos[h] = (g * col).astype(BF16)
        invs.append(inv)

    def grads(n):
        zq, t = place(n)
        k = rows_of(n, 0)
        dk = jnp.zeros((KT, HEAD), F32)
        dv = jnp.zeros((KT, HEAD), F32)
        for h in range(GROUP):
            cols = slice(h * QT, (h + 1) * QT)
            p = pbuf[n, :, cols]
            ds = (p.astype(F32) * (sbuf[n, :, cols] - stat_d[h, :1])).astype(BF16)
            dv += dot(p, dos[h])
            dk += dot(ds, qs[h])
            dqt[h] += dot_tn(k, ds)
        for i in range(PAIR):
            acc[t + i, zq, :, :HEAD] += dk[i * BLK:(i + 1) * BLK]
            acc[t + i, zq, :, HEAD:] += dv[i * BLK:(i + 1) * BLK]

    over_tiles(grads)
    for h in range(GROUP):
        dq_ref[:, h * HEAD:(h + 1) * HEAD] = (dqt[h] * (invs[h] * SCALE)).T.astype(BF16)

    @pl.when(r == NQ - 1)
    def _():
        for i in range(T):
            dkv_ref[i] = acc[i].astype(BF16)


def attention(flags, qd, kv, hot, bias):
    whole = lambda *shape: pl.BlockSpec(shape, lambda r, f: (0,) * len(shape))
    return pl.pallas_call(
        attn_kernel,
        grid_spec=pltpu.PrefetchScalarGridSpec(
            num_scalar_prefetch=1,
            grid=(NQ,),
            in_specs=[
                pl.BlockSpec((QT, 2 * GROUP * HEAD), lambda r, f: (r, 0)),
                whole(T, Z, BLK, 2 * HEAD),
                whole(T, Z, BLK, HEAD),
                pl.BlockSpec((1, HEAD, QT), lambda r, f: (r, 0, 0)),
            ],
            out_specs=[
                pl.BlockSpec((QT, GROUP * HEAD), lambda r, f: (r, 0)),
                whole(T, Z, BLK, 2 * HEAD),
            ],
            scratch_shapes=[
                pltpu.VMEM((T, Z, BLK, 2 * HEAD), F32),
                pltpu.VMEM((NK, KT, GROUP * QT), F32),
                pltpu.VMEM((NK, KT, GROUP * QT), BF16),
                pltpu.VMEM((GROUP, 2 * HEAD, QT), BF16),
                pltpu.VMEM((GROUP, HEAD, QT), BF16),
                pltpu.VMEM((GROUP, QT, HEAD), BF16),
                pltpu.VMEM((GROUP, QT, HEAD), BF16),
                pltpu.VMEM((GROUP, 8, QT), F32),
                pltpu.VMEM((GROUP, 8, QT), F32),
                pltpu.VMEM((GROUP, 8, QT), F32),
                pltpu.VMEM((GROUP, HEAD, QT), F32),
            ],
        ),
        out_shape=[
            jax.ShapeDtypeStruct((Z * BLK, GROUP * HEAD), BF16),
            jax.ShapeDtypeStruct((T, Z, BLK, 2 * HEAD), BF16),
        ],
        compiler_params=pltpu.CompilerParams(
            dimension_semantics=("arbitrary",), vmem_limit_bytes=60 * 1024 * 1024
        ),
    )(flags, qd, kv, hot, bias)


def masks(token_span, visible, t_index):
    spans = token_span.reshape(Z, T, BLK)
    ids = jnp.arange(HEAD, dtype=jnp.int32)
    hot = (spans.transpose(1, 0, 2)[..., None] == ids).astype(BF16)
    mine = lax.dynamic_index_in_dim(spans, t_index, 1, keepdims=False).reshape(NQ, QT)
    span_ids = jnp.arange(visible.shape[0], dtype=jnp.int32)
    mine_hot = (mine[..., None] == span_ids).astype(F32)
    seen = jnp.einsum("rqs,sk->rkq", mine_hot, visible.astype(F32))
    bias = jnp.where(seen > 0, 0.0, NEG).astype(BF16)
    bias = jnp.pad(bias, ((0, 0), (0, HEAD - visible.shape[0]), (0, 0)))
    key_has = jnp.any(token_span.reshape(NK, KT)[..., None] == span_ids, axis=1)
    seen_any = jnp.any(seen > 0, axis=2)
    flags = jnp.any(key_has[None] & seen_any[:, None], axis=2).astype(jnp.int32)
    return hot, bias, flags.reshape(-1)


def per_device(query_rows, key_rows, value_rows, out_grad, token_span, visible):
    t_index = lax.axis_index("y") * C + lax.axis_index("core")
    hot, bias, flags = masks(token_span, visible, t_index)

    def by_head(x):
        return x.reshape(BLK, KV_HEADS, -1).transpose(1, 0, 2)

    def swap(x):
        return lax.all_to_all(x, "z", 0, 0, tiled=True)

    kv = swap(jnp.concatenate([by_head(key_rows), by_head(value_rows)], axis=2))
    kv = lax.all_gather(kv, ("y", "core"), axis=0)
    qd = swap(jnp.concatenate([by_head(query_rows), by_head(out_grad)], axis=2))
    dq, dkv = attention(flags, qd.reshape(Z * BLK, -1), kv, hot, bias)
    dkv = lax.psum_scatter(dkv, ("y", "core"), scatter_dimension=0, tiled=False)
    dkv = swap(dkv).transpose(1, 0, 2)
    dq = swap(dq.reshape(Z, BLK, GROUP * HEAD)).transpose(1, 0, 2).reshape(BLK, HEADS * HEAD)
    dk = dkv[..., :HEAD].reshape(BLK, KV_HEADS * HEAD)
    dv = dkv[..., HEAD:].reshape(BLK, KV_HEADS * HEAD)
    return dq, dk, dv


def solution(mesh):
    dp = mesh.shape["dp"]
    split = Mesh(mesh.devices.reshape(Z, Y, C, dp), ("z", "y", "core", "dp"))
    rows = P(("dp", "z", "y", "core"), None)
    return jax.shard_map(
        per_device,
        mesh=split,
        in_specs=(rows, rows, rows, rows, P("dp"), P("dp", None)),
        out_specs=(rows, rows, rows),
        check_vma=False,
    )
```

```python
import functools

import jax
import jax.numpy as jnp
import numpy as np
from jax import lax
from jax.experimental import pallas as pl
from jax.experimental.pallas import tpu as pltpu
from jax.sharding import Mesh, PartitionSpec as P

HEADS = 12
KV_HEADS = 4
GROUP = HEADS // KV_HEADS
HEAD = 128
SCALE = HEAD ** -0.5
LOG2E = 1.4426950408889634
NEG = -1e30
LEAST = 2.0 ** -60
MOST = 2.0 ** 60
Z, Y, C = 4, 4, 2
T = Y * C
BLK = 192
QT = 256
NQ = Z * BLK // QT
NB = Z * T
WIDE = 4
NI = NB // WIDE
KT = WIDE * BLK
F32 = jnp.float32
BF16 = jnp.bfloat16


def dot(a, b):
    return lax.dot_general(a, b, (((1,), (0,)), ((), ())), preferred_element_type=F32)


def dot_tn(a, b):
    return lax.dot_general(a, b, (((0,), (0,)), ((), ())), preferred_element_type=F32)


def fold(x, op):
    return op(x.reshape(x.shape[0] // 8, 8, x.shape[1]), axis=0)


def attn_kernel(lists, counts, spot, qd_ref, kv_ref, hot_ref, bias_ref, dq_ref, keep_ref, give_ref,
                acc, dpbuf, pbuf, qt, dot_t, qs, dos, stat_m, stat_l, stat_d, dqt):
    r = pl.program_id(0)

    @pl.when(r == 0)
    def _():
        acc[...] = jnp.zeros_like(acc)

    for h in range(GROUP):
        q = qd_ref[:, h * HEAD:(h + 1) * HEAD]
        g = qd_ref[:, (GROUP + h) * HEAD:(GROUP + h + 1) * HEAD]
        qt[h, :HEAD, :] = q.T
        qt[h, HEAD:, :] = bias_ref[0]
        dot_t[h] = g.T
    dqt[...] = jnp.zeros_like(dqt)
    steps = (counts[r] + WIDE - 1) // WIDE

    def blocks(i):
        ids = [lists[r * NB + i * WIDE + j] for j in range(WIDE)]
        real = [jnp.minimum(b, NB - 1) for b in ids]
        return ids, [(b % T, b // T) for b in real]

    def masked_keys(ids, where):
        return jnp.concatenate(
            [jnp.concatenate([kv_ref[t, zq, :, :HEAD], hot_ref[b]], axis=1) for b, (t, zq) in zip(ids, where)],
            axis=0)

    def forward(i, carry):
        ids, where = blocks(i)
        lhs = masked_keys(ids, where)
        v = jnp.concatenate([kv_ref[t, zq, :, HEAD:] for t, zq in where], axis=0)
        for h in range(GROUP):
            cols = slice(h * QT, (h + 1) * QT)
            p = jnp.exp2(dot(lhs, qt[h]) * (SCALE * LOG2E))
            dp = dot(v, dot_t[h])
            stat_l[h] += fold(p, jnp.sum)
            stat_d[h] += fold(p * dp, jnp.sum)
            pbuf[i, :, cols] = p.astype(BF16)
            dpbuf[i, :, cols] = dp
        return carry

    def forward_all():
        stat_l[...] = jnp.zeros_like(stat_l)
        stat_d[...] = jnp.zeros_like(stat_d)
        lax.fori_loop(0, steps, forward, 0)
        return [jnp.sum(stat_l[h], axis=0, keepdims=True) for h in range(GROUP)]

    sums = forward_all()
    least = jnp.min(functools.reduce(jnp.minimum, sums))
    most = jnp.max(functools.reduce(jnp.maximum, sums))

    @pl.when(jnp.logical_not((least > LEAST) & (most < MOST)))
    def _():
        stat_m[...] = jnp.full_like(stat_m, NEG)

        def tops(i, carry):
            lhs = masked_keys(*blocks(i))
            for h in range(GROUP):
                stat_m[h] = jnp.maximum(stat_m[h], fold(dot(lhs, qt[h]), jnp.max))
            return carry

        lax.fori_loop(0, steps, tops, 0)
        for h in range(GROUP):
            top = jnp.max(stat_m[h], axis=0, keepdims=True)
            qt[h, HEAD:, :] = (bias_ref[0].astype(F32) - top).astype(BF16)
        forward_all()

    invs = []
    for h in range(GROUP):
        inv = 1.0 / jnp.sum(stat_l[h], axis=0, keepdims=True)
        delta = jnp.sum(stat_d[h], axis=0, keepdims=True) * inv
        stat_d[h] = jnp.broadcast_to(delta, (8, QT))
        col = jnp.broadcast_to(inv, (HEAD, QT)).T
        q = qd_ref[:, h * HEAD:(h + 1) * HEAD].astype(F32)
        g = qd_ref[:, (GROUP + h) * HEAD:(GROUP + h + 1) * HEAD].astype(F32)
        qs[h * QT:(h + 1) * QT] = (q * (col * SCALE)).astype(BF16)
        dos[h * QT:(h + 1) * QT] = (g * col).astype(BF16)
        invs.append(inv)

    def backward(i, carry):
        _, where = blocks(i)
        k = jnp.concatenate([kv_ref[t, zq, :, :HEAD] for t, zq in where], axis=0)
        dv = dot(pbuf[i], dos[...])
        dss = []
        for h in range(GROUP):
            cols = slice(h * QT, (h + 1) * QT)
            dss.append((pbuf[i, :, cols].astype(F32) * (dpbuf[i, :, cols] - stat_d[h, :1])).astype(BF16))
        ds = jnp.concatenate(dss, axis=1)
        dqt[...] += dot_tn(k, ds)
        dk = dot(ds, qs[...])
        for j, (t, zq) in enumerate(where):
            acc[t, zq, :, :HEAD] += dk[j * BLK:(j + 1) * BLK]
            acc[t, zq, :, HEAD:] += dv[j * BLK:(j + 1) * BLK]
        return carry

    lax.fori_loop(0, steps, backward, 0)
    for h in range(GROUP):
        cols = slice(h * QT, (h + 1) * QT)
        dq_ref[:, h * HEAD:(h + 1) * HEAD] = (dqt[:, cols] * (invs[h] * SCALE)).T.astype(BF16)

    @pl.when(r == NQ - 1)
    def _():
        for i in range(Y):
            keep_ref[i] = acc[i * C + spot[0]].astype(BF16)
            give_ref[i] = acc[i * C + 1 - spot[0]].astype(BF16)


def attention(lists, counts, spot, qd, kv, hot, bias):
    def whole(*shape):
        return pl.BlockSpec(shape, lambda r, *_: (0,) * len(shape))

    return pl.pallas_call(
        attn_kernel,
        grid_spec=pltpu.PrefetchScalarGridSpec(
            num_scalar_prefetch=3,
            grid=(NQ,),
            in_specs=[
                pl.BlockSpec((QT, 2 * GROUP * HEAD), lambda r, *_: (r, 0)),
                whole(T, Z, BLK, 2 * HEAD),
                whole(NB + 1, BLK, HEAD),
                pl.BlockSpec((1, HEAD, QT), lambda r, *_: (r, 0, 0)),
            ],
            out_specs=[
                pl.BlockSpec((QT, GROUP * HEAD), lambda r, *_: (r, 0)),
                whole(Y, Z, BLK, 2 * HEAD),
                whole(Y, Z, BLK, 2 * HEAD),
            ],
            scratch_shapes=[
                pltpu.VMEM((T, Z, BLK, 2 * HEAD), F32),
                pltpu.VMEM((NI, KT, GROUP * QT), F32),
                pltpu.VMEM((NI, KT, GROUP * QT), BF16),
                pltpu.VMEM((GROUP, 2 * HEAD, QT), BF16),
                pltpu.VMEM((GROUP, HEAD, QT), BF16),
                pltpu.VMEM((GROUP * QT, HEAD), BF16),
                pltpu.VMEM((GROUP * QT, HEAD), BF16),
                pltpu.VMEM((GROUP, 8, QT), F32),
                pltpu.VMEM((GROUP, 8, QT), F32),
                pltpu.VMEM((GROUP, 8, QT), F32),
                pltpu.VMEM((HEAD, GROUP * QT), F32),
            ],
        ),
        out_shape=[
            jax.ShapeDtypeStruct((Z * BLK, GROUP * HEAD), BF16),
            jax.ShapeDtypeStruct((Y, Z, BLK, 2 * HEAD), BF16),
            jax.ShapeDtypeStruct((Y, Z, BLK, 2 * HEAD), BF16),
        ],
        compiler_params=pltpu.CompilerParams(
            dimension_semantics=("arbitrary",), vmem_limit_bytes=62 * 1024 * 1024
        ),
    )(lists, counts, spot, qd, kv, hot, bias)


def masks(token_span, visible, t_index):
    spans = token_span.reshape(Z, T, BLK)
    n_spans = visible.shape[0]
    lanes = jnp.arange(HEAD, dtype=jnp.int32)
    empty = jnp.full((1, BLK), n_spans, jnp.int32)
    padded = jnp.concatenate([token_span.reshape(NB, BLK), empty], axis=0)
    hot = (padded[..., None] == lanes).astype(BF16)
    mine = lax.dynamic_index_in_dim(spans, t_index, 1, keepdims=False).reshape(NQ, QT)
    span_ids = jnp.arange(n_spans, dtype=jnp.int32)
    mine_hot = (mine[..., None] == span_ids).astype(F32)
    seen = jnp.einsum("rqs,sk->rkq", mine_hot, visible.astype(F32)) > 0
    bias = jnp.where(seen, 0.0, NEG).astype(BF16)
    bias = jnp.pad(bias, ((0, 0), (0, HEAD - n_spans), (0, 0)), constant_values=NEG)
    key_has = jnp.any(token_span.reshape(NB, BLK)[..., None] == span_ids, axis=1)
    seen_any = jnp.any(seen, axis=2)
    used = jnp.any(key_has[None] & seen_any[:, None], axis=2)
    counts = jnp.sum(used.astype(jnp.int32), axis=1)
    ids = jnp.arange(NB, dtype=jnp.int32)
    rank = jnp.sum((used[:, None, :] & (ids[None, :] <= ids[:, None])).astype(jnp.int32), axis=2) - 1
    here = used[:, None, :] & (rank[:, None, :] == ids[:, None])
    lists = jnp.sum(jnp.where(here, ids, 0), axis=2) + jnp.where(ids >= counts[:, None], NB, 0)
    return hot, bias, lists.reshape(-1).astype(jnp.int32), counts


def per_device(query_rows, key_rows, value_rows, out_grad, token_span, visible):
    core = lax.axis_index("core")
    hot, bias, lists, counts = masks(token_span, visible, lax.axis_index("y") * C + core)

    def by_head(x, y):
        m, n = x.shape[1] // Z, y.shape[1] // Z
        return jnp.stack([jnp.concatenate([x[:, c * m:(c + 1) * m], y[:, c * n:(c + 1) * n]], axis=1) for c in range(Z)])

    def swap(x, axis="z"):
        return lax.all_to_all(x, axis, 0, 0, tiled=True)

    def turn(x):
        me = lax.axis_index("z")
        parts = [lax.dynamic_index_in_dim(x, me, 0, keepdims=False)]
        for k in range(1, Z):
            part = lax.dynamic_index_in_dim(x, (me + k) % Z, 0, keepdims=False)
            parts.append(lax.ppermute(part, "z", [(i, (i + k) % Z) for i in range(Z)]))
        return parts

    def in_order(parts):
        me = lax.axis_index("z")
        parts = jnp.stack(parts)
        return [lax.dynamic_index_in_dim(parts, (me - c) % Z, 0, keepdims=False) for c in range(Z)]

    kv = lax.all_gather(swap(by_head(key_rows, value_rows)), ("y", "core"), axis=0)
    qd = swap(by_head(query_rows, out_grad)).reshape(Z * BLK, -1)
    dq, keep, give = attention(lists, counts, core.reshape(1), qd, kv, hot, bias)
    dq = turn(dq.reshape(Z, BLK, GROUP * HEAD))
    other = lax.ppermute(give, "core", [(0, 1), (1, 0)])
    dkv = swap((keep.astype(F32) + other.astype(F32)).astype(BF16), "y")
    dkv, dq = lax.optimization_barrier((dkv, dq))
    dkv = swap(jnp.sum(dkv.astype(F32), axis=0).astype(BF16))
    dq = jnp.concatenate(in_order(dq), axis=1)
    dk = jnp.concatenate([dkv[c, :, :HEAD] for c in range(Z)], axis=1)
    dv = jnp.concatenate([dkv[c, :, HEAD:] for c in range(Z)], axis=1)
    return dq, dk, dv


def solution(mesh):
    dp = mesh.shape["dp"]
    split = Mesh(mesh.devices.reshape(Z, Y, C, dp), ("z", "y", "core", "dp"))
    rows = P(("dp", "z", "y", "core"), None)
    return jax.shard_map(
        per_device,
        mesh=split,
        in_specs=(rows, rows, rows, rows, P("dp"), P("dp", None)),
        out_specs=(rows, rows, rows),
        check_vma=False,
    )
```

```python
import functools

import jax
import jax.numpy as jnp
import numpy as np
from jax import lax
from jax.experimental import pallas as pl
from jax.experimental.pallas import tpu as pltpu
from jax.sharding import Mesh, PartitionSpec as P

HEADS = 12
KV_HEADS = 4
GROUP = HEADS // KV_HEADS
HEAD = 128
SCALE = HEAD ** -0.5
LOG2E = 1.4426950408889634
NEG = -1e30
LIMIT = 48
LEAST = 2.0 ** -60
MOST = 2.0 ** 60
Z, Y, C = 4, 4, 2
T = Y * C
BLK = 192
QT = 256
NQ = Z * BLK // QT
NB = Z * T
WIDE = 4
NI = NB // WIDE
KT = WIDE * BLK
F32 = jnp.float32
BF16 = jnp.bfloat16


def dot(a, b):
    return lax.dot_general(a, b, (((1,), (0,)), ((), ())), preferred_element_type=F32)


def dot_tn(a, b):
    return lax.dot_general(a, b, (((0,), (0,)), ((), ())), preferred_element_type=F32)


def fold(x, op):
    return op(x.reshape(x.shape[0] // 8, 8, x.shape[1]), axis=0)


def attn_kernel(lists, counts, spot, qd_all, kv_ref, hot_ref, bias_ref, dq_ref, keep_ref, give_ref,
                acc, dpbuf, pbuf, qt, dot_t, qs, dos, stat_m, stat_l, stat_d, dqt):
    r = pl.program_id(0)
    qd_ref = qd_all.at[pl.ds(pl.multiple_of(r * QT, QT), QT)]

    @pl.when(r == 0)
    def _():
        acc[...] = jnp.zeros_like(acc)

    for h in range(GROUP):
        q = qd_ref[:, h * HEAD:(h + 1) * HEAD]
        g = qd_ref[:, (GROUP + h) * HEAD:(GROUP + h + 1) * HEAD]
        qt[h, :HEAD, :] = q.T
        qt[h, HEAD:, :] = bias_ref[r]
        dot_t[h] = g.T
    dqt[...] = jnp.zeros_like(dqt)
    steps = (counts[r] + WIDE - 1) // WIDE

    def blocks(i):
        ids = [lists[r * NB + i * WIDE + j] for j in range(WIDE)]
        real = [jnp.minimum(b, NB - 1) for b in ids]
        return ids, [(b % T, b // T) for b in real]

    def masked_keys(ids, where):
        return jnp.concatenate(
            [jnp.concatenate([kv_ref[t, zq, :, :HEAD], hot_ref[b]], axis=1) for b, (t, zq) in zip(ids, where)],
            axis=0)

    def forward(i, carry):
        ids, where = blocks(i)
        lhs = masked_keys(ids, where)
        v = jnp.concatenate([kv_ref[t, zq, :, HEAD:] for t, zq in where], axis=0)
        for h in range(GROUP):
            cols = slice(h * QT, (h + 1) * QT)
            p = jnp.exp2(dot(lhs, qt[h]) * (SCALE * LOG2E))
            dp = dot(v, dot_t[h])
            stat_l[h] += fold(p, jnp.sum)
            stat_d[h] += fold(p * dp, jnp.sum)
            pbuf[i, :, cols] = p.astype(BF16)
            dpbuf[i, :, cols] = dp
        return carry

    def forward_all():
        stat_l[...] = jnp.zeros_like(stat_l)
        stat_d[...] = jnp.zeros_like(stat_d)
        lax.fori_loop(0, steps, forward, 0)
        return [jnp.sum(stat_l[h], axis=0, keepdims=True) for h in range(GROUP)]

    sums = forward_all()
    least = jnp.min(functools.reduce(jnp.minimum, sums))
    most = jnp.max(functools.reduce(jnp.maximum, sums))

    @pl.when(jnp.logical_not((least > LEAST) & (most < MOST)))
    def _():
        stat_m[...] = jnp.full_like(stat_m, NEG)

        def tops(i, carry):
            lhs = masked_keys(*blocks(i))
            for h in range(GROUP):
                stat_m[h] = jnp.maximum(stat_m[h], fold(dot(lhs, qt[h]), jnp.max))
            return carry

        lax.fori_loop(0, steps, tops, 0)
        for h in range(GROUP):
            top = jnp.max(stat_m[h], axis=0, keepdims=True)
            qt[h, HEAD:, :] = (bias_ref[r].astype(F32) - top).astype(BF16)
        forward_all()

    invs = []
    for h in range(GROUP):
        inv = 1.0 / jnp.sum(stat_l[h], axis=0, keepdims=True)
        delta = jnp.sum(stat_d[h], axis=0, keepdims=True) * inv
        stat_d[h] = jnp.broadcast_to(delta, (8, QT))
        col = jnp.broadcast_to(inv, (HEAD, QT)).T
        q = qd_ref[:, h * HEAD:(h + 1) * HEAD].astype(F32)
        g = qd_ref[:, (GROUP + h) * HEAD:(GROUP + h + 1) * HEAD].astype(F32)
        qs[h * QT:(h + 1) * QT] = (q * (col * SCALE)).astype(BF16)
        dos[h * QT:(h + 1) * QT] = (g * col).astype(BF16)
        invs.append(inv)

    def backward(i, carry):
        _, where = blocks(i)
        k = jnp.concatenate([kv_ref[t, zq, :, :HEAD] for t, zq in where], axis=0)
        dv = dot(pbuf[i], dos[...])
        dss = []
        for h in range(GROUP):
            cols = slice(h * QT, (h + 1) * QT)
            dss.append((pbuf[i, :, cols].astype(F32) * (dpbuf[i, :, cols] - stat_d[h, :1])).astype(BF16))
        ds = jnp.concatenate(dss, axis=1)
        dqt[...] += dot_tn(k, ds)
        dk = dot(ds, qs[...])
        for j, (t, zq) in enumerate(where):
            acc[t, zq, :, :HEAD] += dk[j * BLK:(j + 1) * BLK]
            acc[t, zq, :, HEAD:] += dv[j * BLK:(j + 1) * BLK]
        return carry

    lax.fori_loop(0, steps, backward, 0)
    for tile in range(NQ):
        @pl.when(r == tile)
        def _():
            for h in range(GROUP):
                cols = slice(h * QT, (h + 1) * QT)
                dq = (dqt[:, cols] * (invs[h] * SCALE)).T.astype(BF16)
                row = 0
                while row < QT:
                    q, start = divmod(tile * QT + row, BLK)
                    take = min(BLK - start, QT - row)
                    dq_ref[(q + Z - spot[1]) % Z, start:start + take, h * HEAD:(h + 1) * HEAD] = dq[row:row + take]
                    row += take

    @pl.when(r == NQ - 1)
    def _():
        for i in range(Y):
            keep_ref[i] = acc[i * C + spot[0]].astype(BF16)
            give_ref[i] = acc[i * C + 1 - spot[0]].astype(BF16)


def attention(lists, counts, spot, qd, kv, hot, bias):
    vmem = pl.BlockSpec(memory_space=pltpu.VMEM)
    return pl.pallas_call(
        attn_kernel,
        grid_spec=pltpu.PrefetchScalarGridSpec(
            num_scalar_prefetch=3,
            grid=(NQ,),
            in_specs=[vmem] * 4,
            out_specs=[vmem] * 3,
            scratch_shapes=[
                pltpu.VMEM((T, Z, BLK, 2 * HEAD), F32),
                pltpu.VMEM((NI, KT, GROUP * QT), F32),
                pltpu.VMEM((NI, KT, GROUP * QT), BF16),
                pltpu.VMEM((GROUP, 2 * HEAD, QT), BF16),
                pltpu.VMEM((GROUP, HEAD, QT), BF16),
                pltpu.VMEM((GROUP * QT, HEAD), BF16),
                pltpu.VMEM((GROUP * QT, HEAD), BF16),
                pltpu.VMEM((GROUP, 8, QT), F32),
                pltpu.VMEM((GROUP, 8, QT), F32),
                pltpu.VMEM((GROUP, 8, QT), F32),
                pltpu.VMEM((HEAD, GROUP * QT), F32),
            ],
        ),
        out_shape=[
            jax.ShapeDtypeStruct((Z, BLK, GROUP * HEAD), BF16),
            jax.ShapeDtypeStruct((Y, Z, BLK, 2 * HEAD), BF16),
            jax.ShapeDtypeStruct((Y, Z, BLK, 2 * HEAD), BF16),
        ],
        compiler_params=pltpu.CompilerParams(
            dimension_semantics=("arbitrary",), vmem_limit_bytes=LIMIT * 1024 * 1024
        ),
    )(lists, counts, spot, qd, kv, hot, bias)


def masks(token_span, visible, t_index):
    spans = token_span.reshape(Z, T, BLK)
    n_spans = visible.shape[0]
    lanes = jnp.arange(HEAD, dtype=jnp.int32)
    empty = jnp.full((1, BLK), n_spans, jnp.int32)
    padded = jnp.concatenate([token_span.reshape(NB, BLK), empty], axis=0)
    hot = (padded[..., None] == lanes).astype(BF16)
    mine = lax.dynamic_index_in_dim(spans, t_index, 1, keepdims=False).reshape(NQ, QT)
    span_ids = jnp.arange(n_spans, dtype=jnp.int32)
    mine_hot = (mine[..., None] == span_ids).astype(F32)
    seen = jnp.einsum("rqs,sk->rkq", mine_hot, visible.astype(F32)) > 0
    bias = jnp.where(seen, 0.0, NEG).astype(BF16)
    bias = jnp.pad(bias, ((0, 0), (0, HEAD - n_spans), (0, 0)), constant_values=NEG)
    key_has = jnp.any(token_span.reshape(NB, BLK)[..., None] == span_ids, axis=1)
    seen_any = jnp.any(seen, axis=2)
    used = jnp.any(key_has[None] & seen_any[:, None], axis=2)
    counts = jnp.sum(used.astype(jnp.int32), axis=1)
    ids = jnp.arange(NB, dtype=jnp.int32)
    rank = jnp.sum((used[:, None, :] & (ids[None, :] <= ids[:, None])).astype(jnp.int32), axis=2) - 1
    here = used[:, None, :] & (rank[:, None, :] == ids[:, None])
    lists = jnp.sum(jnp.where(here, ids, 0), axis=2) + jnp.where(ids >= counts[:, None], NB, 0)
    return hot, bias, lists.reshape(-1).astype(jnp.int32), counts


def per_device(query_rows, key_rows, value_rows, out_grad, token_span, visible):
    core = lax.axis_index("core")
    hot, bias, lists, counts = masks(token_span, visible, lax.axis_index("y") * C + core)

    def by_head(x, y):
        m, n = x.shape[1] // Z, y.shape[1] // Z
        return jnp.stack([jnp.concatenate([x[:, c * m:(c + 1) * m], y[:, c * n:(c + 1) * n]], axis=1) for c in range(Z)])

    def swap(x, axis="z"):
        return lax.all_to_all(x, axis, 0, 0, tiled=True)

    def turn(x):
        return [x[0]] + [lax.ppermute(x[k], "z", [(i, (i + k) % Z) for i in range(Z)]) for k in range(1, Z)]

    def in_order(parts):
        me = lax.axis_index("z")
        parts = jnp.stack(parts)
        return [lax.dynamic_index_in_dim(parts, (me - c) % Z, 0, keepdims=False) for c in range(Z)]

    kv = lax.all_gather(swap(by_head(key_rows, value_rows)), ("y", "core"), axis=0)
    qd = swap(by_head(query_rows, out_grad)).reshape(Z * BLK, -1)
    dq, keep, give = attention(lists, counts, jnp.stack([core, lax.axis_index("z")]), qd, kv, hot, bias)
    dq = turn(dq)
    other = lax.ppermute(give, "core", [(0, 1), (1, 0)])
    dkv = swap((keep.astype(F32) + other.astype(F32)).astype(BF16), "y")
    dkv, dq = lax.optimization_barrier((dkv, dq))
    dkv = swap(jnp.sum(dkv.astype(F32), axis=0).astype(BF16))
    dq = jnp.concatenate(in_order(dq), axis=1)
    dk = jnp.concatenate([dkv[c, :, :HEAD] for c in range(Z)], axis=1)
    dv = jnp.concatenate([dkv[c, :, HEAD:] for c in range(Z)], axis=1)
    return dq, dk, dv


def solution(mesh):
    dp = mesh.shape["dp"]
    split = Mesh(mesh.devices.reshape(Z, Y, C, dp), ("z", "y", "core", "dp"))
    rows = P(("dp", "z", "y", "core"), None)
    return jax.shard_map(
        per_device,
        mesh=split,
        in_specs=(rows, rows, rows, rows, P("dp"), P("dp", None)),
        out_specs=(rows, rows, rows),
        check_vma=False,
    )
```

```python
import functools

import jax
import jax.numpy as jnp
import numpy as np
from jax import lax
from jax.experimental import pallas as pl
from jax.experimental.pallas import tpu as pltpu
from jax.sharding import Mesh, PartitionSpec as P

HEADS = 12
KV_HEADS = 4
GROUP = HEADS // KV_HEADS
HEAD = 128
SCALE = HEAD ** -0.5
LOG2E = 1.4426950408889634
NEG = -1e30
LIMIT = 48
LEAST = 2.0 ** -60
MOST = 2.0 ** 60
Z, Y, C = 4, 4, 2
T = Y * C
BLK = 192
QT = 256
NQ = Z * BLK // QT
NB = Z * T
WIDE = 4
NI = NB // WIDE
KT = WIDE * BLK
F32 = jnp.float32
BF16 = jnp.bfloat16


def dot(a, b):
    return lax.dot_general(a, b, (((1,), (0,)), ((), ())), preferred_element_type=F32)


def dot_tn(a, b):
    return lax.dot_general(a, b, (((0,), (0,)), ((), ())), preferred_element_type=F32)


def fold(x, op):
    return op(x.reshape(x.shape[0] // 8, 8, x.shape[1]), axis=0)


def attn_kernel(lists, counts, spot, qd_all, kv_ref, hot_ref, bias_ref, dq_ref, keep_ref, give_ref,
                acc, dpbuf, pbuf, qt, dot_t, qs, dos, stat_m, stat_l, stat_d, dqt):
    r = pl.program_id(0)
    qd_ref = qd_all.at[pl.ds(pl.multiple_of(r * QT, QT), QT)]

    @pl.when(r == 0)
    def _():
        acc[...] = jnp.zeros_like(acc)

    for h in range(GROUP):
        q = qd_ref[:, h * HEAD:(h + 1) * HEAD]
        g = qd_ref[:, (GROUP + h) * HEAD:(GROUP + h + 1) * HEAD]
        qt[h, :HEAD, :] = q.T
        qt[h, HEAD:, :] = bias_ref[r]
        dot_t[h] = g.T
    dqt[...] = jnp.zeros_like(dqt)
    steps = (counts[r] + WIDE - 1) // WIDE

    def blocks(i):
        ids = [lists[r * NB + i * WIDE + j] for j in range(WIDE)]
        real = [jnp.minimum(b, NB - 1) for b in ids]
        return ids, [(b % T, b // T) for b in real]

    def masked_keys(ids, where):
        return jnp.concatenate(
            [jnp.concatenate([kv_ref[t, zq, :, :HEAD], hot_ref[b]], axis=1) for b, (t, zq) in zip(ids, where)],
            axis=0)

    def forward(i, carry):
        ids, where = blocks(i)
        lhs = masked_keys(ids, where)
        v = jnp.concatenate([kv_ref[t, zq, :, HEAD:] for t, zq in where], axis=0)
        for h in range(GROUP):
            cols = slice(h * QT, (h + 1) * QT)
            p = jnp.exp2(dot(lhs, qt[h]) * (SCALE * LOG2E))
            dp = dot(v, dot_t[h])
            stat_l[h] += fold(p, jnp.sum)
            stat_d[h] += fold(p * dp, jnp.sum)
            pbuf[i, :, cols] = p.astype(BF16)
            dpbuf[i, :, cols] = dp
        return carry

    def forward_all():
        stat_l[...] = jnp.zeros_like(stat_l)
        stat_d[...] = jnp.zeros_like(stat_d)
        lax.fori_loop(0, steps, forward, 0)
        return [jnp.sum(stat_l[h], axis=0, keepdims=True) for h in range(GROUP)]

    sums = forward_all()
    least = jnp.min(functools.reduce(jnp.minimum, sums))
    most = jnp.max(functools.reduce(jnp.maximum, sums))

    @pl.when(jnp.logical_not((least > LEAST) & (most < MOST)))
    def _():
        stat_m[...] = jnp.full_like(stat_m, NEG)

        def tops(i, carry):
            lhs = masked_keys(*blocks(i))
            for h in range(GROUP):
                stat_m[h] = jnp.maximum(stat_m[h], fold(dot(lhs, qt[h]), jnp.max))
            return carry

        lax.fori_loop(0, steps, tops, 0)
        for h in range(GROUP):
            top = jnp.max(stat_m[h], axis=0, keepdims=True)
            qt[h, HEAD:, :] = (bias_ref[r].astype(F32) - top).astype(BF16)
        forward_all()

    invs = []
    for h in range(GROUP):
        inv = 1.0 / jnp.sum(stat_l[h], axis=0, keepdims=True)
        delta = jnp.sum(stat_d[h], axis=0, keepdims=True) * inv
        stat_d[h] = jnp.broadcast_to(delta, (8, QT))
        col = jnp.broadcast_to(inv, (HEAD, QT)).T
        q = qd_ref[:, h * HEAD:(h + 1) * HEAD].astype(F32)
        g = qd_ref[:, (GROUP + h) * HEAD:(GROUP + h + 1) * HEAD].astype(F32)
        qs[h * QT:(h + 1) * QT] = (q * (col * SCALE)).astype(BF16)
        dos[h * QT:(h + 1) * QT] = (g * col).astype(BF16)
        invs.append(inv)

    def backward(i, carry):
        _, where = blocks(i)
        k = jnp.concatenate([kv_ref[t, zq, :, :HEAD] for t, zq in where], axis=0)
        dv = dot(pbuf[i], dos[...])
        dss = []
        for h in range(GROUP):
            cols = slice(h * QT, (h + 1) * QT)
            dss.append((pbuf[i, :, cols].astype(F32) * (dpbuf[i, :, cols] - stat_d[h, :1])).astype(BF16))
        ds = jnp.concatenate(dss, axis=1)
        dqt[...] += dot_tn(k, ds)
        dk = dot(ds, qs[...])
        for j, (t, zq) in enumerate(where):
            acc[t, zq, :, :HEAD] += dk[j * BLK:(j + 1) * BLK]
            acc[t, zq, :, HEAD:] += dv[j * BLK:(j + 1) * BLK]
        return carry

    lax.fori_loop(0, steps, backward, 0)
    for tile in range(NQ):
        @pl.when(r == tile)
        def _():
            for h in range(GROUP):
                cols = slice(h * QT, (h + 1) * QT)
                dq = (dqt[:, cols] * (invs[h] * SCALE)).T.astype(BF16)
                row = 0
                while row < QT:
                    q, start = divmod(tile * QT + row, BLK)
                    take = min(BLK - start, QT - row)
                    dq_ref[q, start:start + take, h * HEAD:(h + 1) * HEAD] = dq[row:row + take]
                    row += take

    @pl.when(r == NQ - 1)
    def _():
        for i in range(Y):
            y = (spot[1] + i) % Y
            keep_ref[i] = acc[y * C + spot[0]].astype(BF16)
            give_ref[i] = acc[y * C + 1 - spot[0]].astype(BF16)


def attention(lists, counts, spot, qd, kv, hot, bias):
    vmem = pl.BlockSpec(memory_space=pltpu.VMEM)
    return pl.pallas_call(
        attn_kernel,
        grid_spec=pltpu.PrefetchScalarGridSpec(
            num_scalar_prefetch=3,
            grid=(NQ,),
            in_specs=[vmem] * 4,
            out_specs=[vmem] * 3,
            scratch_shapes=[
                pltpu.VMEM((T, Z, BLK, 2 * HEAD), F32),
                pltpu.VMEM((NI, KT, GROUP * QT), F32),
                pltpu.VMEM((NI, KT, GROUP * QT), BF16),
                pltpu.VMEM((GROUP, 2 * HEAD, QT), BF16),
                pltpu.VMEM((GROUP, HEAD, QT), BF16),
                pltpu.VMEM((GROUP * QT, HEAD), BF16),
                pltpu.VMEM((GROUP * QT, HEAD), BF16),
                pltpu.VMEM((GROUP, 8, QT), F32),
                pltpu.VMEM((GROUP, 8, QT), F32),
                pltpu.VMEM((GROUP, 8, QT), F32),
                pltpu.VMEM((HEAD, GROUP * QT), F32),
            ],
        ),
        out_shape=[
            jax.ShapeDtypeStruct((Z, BLK, GROUP * HEAD), BF16),
            jax.ShapeDtypeStruct((Y, Z, BLK, 2 * HEAD), BF16),
            jax.ShapeDtypeStruct((Y, Z, BLK, 2 * HEAD), BF16),
        ],
        compiler_params=pltpu.CompilerParams(
            dimension_semantics=("arbitrary",), vmem_limit_bytes=LIMIT * 1024 * 1024
        ),
    )(lists, counts, spot, qd, kv, hot, bias)


def masks(token_span, visible, t_index):
    spans = token_span.reshape(Z, T, BLK)
    n_spans = visible.shape[0]
    lanes = jnp.arange(HEAD, dtype=jnp.int32)
    empty = jnp.full((1, BLK), n_spans, jnp.int32)
    padded = jnp.concatenate([token_span.reshape(NB, BLK), empty], axis=0)
    hot = (padded[..., None] == lanes).astype(BF16)
    mine = lax.dynamic_index_in_dim(spans, t_index, 1, keepdims=False).reshape(NQ, QT)
    span_ids = jnp.arange(n_spans, dtype=jnp.int32)
    mine_hot = (mine[..., None] == span_ids).astype(F32)
    seen = jnp.einsum("rqs,sk->rkq", mine_hot, visible.astype(F32)) > 0
    bias = jnp.where(seen, 0.0, NEG).astype(BF16)
    bias = jnp.pad(bias, ((0, 0), (0, HEAD - n_spans), (0, 0)), constant_values=NEG)
    key_has = jnp.any(token_span.reshape(NB, BLK)[..., None] == span_ids, axis=1)
    seen_any = jnp.any(seen, axis=2)
    used = jnp.any(key_has[None] & seen_any[:, None], axis=2)
    counts = jnp.sum(used.astype(jnp.int32), axis=1)
    ids = jnp.arange(NB, dtype=jnp.int32)
    rank = jnp.sum((used[:, None, :] & (ids[None, :] <= ids[:, None])).astype(jnp.int32), axis=2) - 1
    here = used[:, None, :] & (rank[:, None, :] == ids[:, None])
    lists = jnp.sum(jnp.where(here, ids, 0), axis=2) + jnp.where(ids >= counts[:, None], NB, 0)
    return hot, bias, lists.reshape(-1).astype(jnp.int32), counts


def per_device(query_rows, key_rows, value_rows, out_grad, token_span, visible):
    core = lax.axis_index("core")
    hot, bias, lists, counts = masks(token_span, visible, lax.axis_index("y") * C + core)

    def by_head(x, y):
        m, n = x.shape[1] // Z, y.shape[1] // Z
        return jnp.stack([jnp.concatenate([x[:, c * m:(c + 1) * m], y[:, c * n:(c + 1) * n]], axis=1) for c in range(Z)])

    def swap(x, axis="z"):
        return lax.all_to_all(x, axis, 0, 0, tiled=True)

    def shift(x, axis, size, k):
        return lax.ppermute(x, axis, [(i, (i + k) % size) for i in range(size)])

    kv = lax.all_gather(swap(by_head(key_rows, value_rows)), ("y", "core"), axis=0)
    qd = swap(by_head(query_rows, out_grad)).reshape(Z * BLK, -1)
    dq, keep, give = attention(lists, counts, jnp.stack([core, lax.axis_index("y")]), qd, kv, hot, bias)
    dq = swap(dq)
    other = shift(give, "core", C, 1)
    both = [(keep[k].astype(F32) + other[k].astype(F32)).astype(BF16) for k in range(Y)]
    parts = [both[0]] + [shift(both[k], "y", Y, k) for k in range(1, Y)]
    parts, dq = lax.optimization_barrier((parts, dq))
    dkv = functools.reduce(jnp.add, [part.astype(F32) for part in parts]).astype(BF16)
    dkv = swap(dkv)
    dq = jnp.concatenate([dq[c] for c in range(Z)], axis=1)
    dk = jnp.concatenate([dkv[c, :, :HEAD] for c in range(Z)], axis=1)
    dv = jnp.concatenate([dkv[c, :, HEAD:] for c in range(Z)], axis=1)
    return dq, dk, dv


def solution(mesh):
    dp = mesh.shape["dp"]
    split = Mesh(mesh.devices.reshape(Z, Y, C, dp), ("z", "y", "core", "dp"))
    rows = P(("dp", "z", "y", "core"), None)
    return jax.shard_map(
        per_device,
        mesh=split,
        in_specs=(rows, rows, rows, rows, P("dp"), P("dp", None)),
        out_specs=(rows, rows, rows),
        check_vma=False,
    )
```

```python
import functools

import jax
import jax.numpy as jnp
import numpy as np
from jax import lax
from jax.experimental import pallas as pl
from jax.experimental.pallas import tpu as pltpu
from jax.sharding import Mesh, PartitionSpec as P

HEADS = 12
KV_HEADS = 4
GROUP = HEADS // KV_HEADS
HEAD = 128
SCALE = HEAD ** -0.5
LOG2E = 1.4426950408889634
NEG = -1e30
LIMIT = 48
LEAST = 2.0 ** -60
MOST = 2.0 ** 60
Z, Y, C = 4, 4, 2
T = Y * C
BLK = 192
QT = 256
NQ = Z * BLK // QT
NB = Z * T
WIDE = 4
NI = NB // WIDE
KT = WIDE * BLK
F32 = jnp.float32
BF16 = jnp.bfloat16


def dot(a, b):
    return lax.dot_general(a, b, (((1,), (0,)), ((), ())), preferred_element_type=F32)


def dot_tn(a, b):
    return lax.dot_general(a, b, (((0,), (0,)), ((), ())), preferred_element_type=F32)


def fold(x, op):
    return op(x.reshape(x.shape[0] // 8, 8, x.shape[1]), axis=0)


def attn_kernel(lists, counts, spot, qd0, qd1, qd2, qd3, kv_ref, hot_ref, bias_ref, dq_ref, keep_ref, give_ref,
                qd_all, acc, dpbuf, pbuf, qt, dot_t, qs, dos, stat_m, stat_l, stat_d, dqt):
    r = pl.program_id(0)

    def slot(q):
        return (spot[2] + Z - q) % Z

    qd_ref = qd_all.at[pl.ds(pl.multiple_of(r * QT, QT), QT)]

    @pl.when(r == 0)
    def _():
        acc[...] = jnp.zeros_like(acc)
        for k, part in enumerate((qd0, qd1, qd2, qd3)):
            qd_all[pl.ds(pl.multiple_of(slot(k) * BLK, BLK), BLK)] = part[...]

    for h in range(GROUP):
        q = qd_ref[:, h * HEAD:(h + 1) * HEAD]
        g = qd_ref[:, (GROUP + h) * HEAD:(GROUP + h + 1) * HEAD]
        qt[h, :HEAD, :] = q.T
        qt[h, HEAD:, :] = bias_ref[r]
        dot_t[h] = g.T
    dqt[...] = jnp.zeros_like(dqt)
    steps = (counts[r] + WIDE - 1) // WIDE

    def blocks(i):
        ids = [lists[r * NB + i * WIDE + j] for j in range(WIDE)]
        real = [jnp.minimum(b, NB - 1) for b in ids]
        return ids, [(b % T, slot(b // T)) for b in real]

    def masked_keys(ids, where):
        return jnp.concatenate(
            [jnp.concatenate([kv_ref[t, zq, :, :HEAD], hot_ref[b]], axis=1) for b, (t, zq) in zip(ids, where)],
            axis=0)

    def forward(i, carry):
        ids, where = blocks(i)
        lhs = masked_keys(ids, where)
        v = jnp.concatenate([kv_ref[t, zq, :, HEAD:] for t, zq in where], axis=0)
        for h in range(GROUP):
            cols = slice(h * QT, (h + 1) * QT)
            p = jnp.exp2(dot(lhs, qt[h]) * (SCALE * LOG2E))
            dp = dot(v, dot_t[h])
            stat_l[h] += fold(p, jnp.sum)
            stat_d[h] += fold(p * dp, jnp.sum)
            pbuf[i, :, cols] = p.astype(BF16)
            dpbuf[i, :, cols] = dp
        return carry

    def forward_all():
        stat_l[...] = jnp.zeros_like(stat_l)
        stat_d[...] = jnp.zeros_like(stat_d)
        lax.fori_loop(0, steps, forward, 0)
        return [jnp.sum(stat_l[h], axis=0, keepdims=True) for h in range(GROUP)]

    sums = forward_all()
    least = jnp.min(functools.reduce(jnp.minimum, sums))
    most = jnp.max(functools.reduce(jnp.maximum, sums))

    @pl.when(jnp.logical_not((least > LEAST) & (most < MOST)))
    def _():
        stat_m[...] = jnp.full_like(stat_m, NEG)

        def tops(i, carry):
            lhs = masked_keys(*blocks(i))
            for h in range(GROUP):
                stat_m[h] = jnp.maximum(stat_m[h], fold(dot(lhs, qt[h]), jnp.max))
            return carry

        lax.fori_loop(0, steps, tops, 0)
        for h in range(GROUP):
            top = jnp.max(stat_m[h], axis=0, keepdims=True)
            qt[h, HEAD:, :] = (bias_ref[r].astype(F32) - top).astype(BF16)
        forward_all()

    invs = []
    for h in range(GROUP):
        inv = 1.0 / jnp.sum(stat_l[h], axis=0, keepdims=True)
        delta = jnp.sum(stat_d[h], axis=0, keepdims=True) * inv
        stat_d[h] = jnp.broadcast_to(delta, (8, QT))
        col = jnp.broadcast_to(inv, (HEAD, QT)).T
        q = qd_ref[:, h * HEAD:(h + 1) * HEAD].astype(F32)
        g = qd_ref[:, (GROUP + h) * HEAD:(GROUP + h + 1) * HEAD].astype(F32)
        qs[h * QT:(h + 1) * QT] = (q * (col * SCALE)).astype(BF16)
        dos[h * QT:(h + 1) * QT] = (g * col).astype(BF16)
        invs.append(inv)

    def backward(i, carry):
        _, where = blocks(i)
        k = jnp.concatenate([kv_ref[t, zq, :, :HEAD] for t, zq in where], axis=0)
        dv = dot(pbuf[i], dos[...])
        dss = []
        for h in range(GROUP):
            cols = slice(h * QT, (h + 1) * QT)
            dss.append((pbuf[i, :, cols].astype(F32) * (dpbuf[i, :, cols] - stat_d[h, :1])).astype(BF16))
        ds = jnp.concatenate(dss, axis=1)
        dqt[...] += dot_tn(k, ds)
        dk = dot(ds, qs[...])
        for j, (t, zq) in enumerate(where):
            acc[t, zq, :, :HEAD] += dk[j * BLK:(j + 1) * BLK]
            acc[t, zq, :, HEAD:] += dv[j * BLK:(j + 1) * BLK]
        return carry

    lax.fori_loop(0, steps, backward, 0)
    for tile in range(NQ):
        @pl.when(r == tile)
        def _():
            for h in range(GROUP):
                cols = slice(h * QT, (h + 1) * QT)
                dq = (dqt[:, cols] * (invs[h] * SCALE)).T.astype(BF16)
                row = 0
                while row < QT:
                    q, start = divmod(tile * QT + row, BLK)
                    take = min(BLK - start, QT - row)
                    dq_ref[slot(q), start:start + take, h * HEAD:(h + 1) * HEAD] = dq[row:row + take]
                    row += take

    @pl.when(r == NQ - 1)
    def _():
        for i in range(Y):
            y = (spot[1] + i) % Y
            keep_ref[i] = acc[y * C + spot[0]].astype(BF16)
            give_ref[i] = acc[y * C + 1 - spot[0]].astype(BF16)


def attention(lists, counts, spot, qd_parts, kv, hot, bias):
    vmem = pl.BlockSpec(memory_space=pltpu.VMEM)
    return pl.pallas_call(
        attn_kernel,
        grid_spec=pltpu.PrefetchScalarGridSpec(
            num_scalar_prefetch=3,
            grid=(NQ,),
            in_specs=[vmem] * (Z + 3),
            out_specs=[vmem] * 3,
            scratch_shapes=[
                pltpu.VMEM((Z * BLK, 2 * GROUP * HEAD), BF16),
                pltpu.VMEM((T, Z, BLK, 2 * HEAD), F32),
                pltpu.VMEM((NI, KT, GROUP * QT), F32),
                pltpu.VMEM((NI, KT, GROUP * QT), BF16),
                pltpu.VMEM((GROUP, 2 * HEAD, QT), BF16),
                pltpu.VMEM((GROUP, HEAD, QT), BF16),
                pltpu.VMEM((GROUP * QT, HEAD), BF16),
                pltpu.VMEM((GROUP * QT, HEAD), BF16),
                pltpu.VMEM((GROUP, 8, QT), F32),
                pltpu.VMEM((GROUP, 8, QT), F32),
                pltpu.VMEM((GROUP, 8, QT), F32),
                pltpu.VMEM((HEAD, GROUP * QT), F32),
            ],
        ),
        out_shape=[
            jax.ShapeDtypeStruct((Z, BLK, GROUP * HEAD), BF16),
            jax.ShapeDtypeStruct((Y, Z, BLK, 2 * HEAD), BF16),
            jax.ShapeDtypeStruct((Y, Z, BLK, 2 * HEAD), BF16),
        ],
        compiler_params=pltpu.CompilerParams(
            dimension_semantics=("arbitrary",), vmem_limit_bytes=LIMIT * 1024 * 1024
        ),
    )(lists, counts, spot, *qd_parts, kv, hot, bias)


def masks(token_span, visible, t_index):
    spans = token_span.reshape(Z, T, BLK)
    n_spans = visible.shape[0]
    lanes = jnp.arange(HEAD, dtype=jnp.int32)
    empty = jnp.full((1, BLK), n_spans, jnp.int32)
    padded = jnp.concatenate([token_span.reshape(NB, BLK), empty], axis=0)
    hot = (padded[..., None] == lanes).astype(BF16)
    mine = lax.dynamic_index_in_dim(spans, t_index, 1, keepdims=False).reshape(NQ, QT)
    span_ids = jnp.arange(n_spans, dtype=jnp.int32)
    mine_hot = (mine[..., None] == span_ids).astype(F32)
    seen = jnp.einsum("rqs,sk->rkq", mine_hot, visible.astype(F32)) > 0
    bias = jnp.where(seen, 0.0, NEG).astype(BF16)
    bias = jnp.pad(bias, ((0, 0), (0, HEAD - n_spans), (0, 0)), constant_values=NEG)
    key_has = jnp.any(token_span.reshape(NB, BLK)[..., None] == span_ids, axis=1)
    seen_any = jnp.any(seen, axis=2)
    used = jnp.any(key_has[None] & seen_any[:, None], axis=2)
    counts = jnp.sum(used.astype(jnp.int32), axis=1)
    ids = jnp.arange(NB, dtype=jnp.int32)
    rank = jnp.sum((used[:, None, :] & (ids[None, :] <= ids[:, None])).astype(jnp.int32), axis=2) - 1
    here = used[:, None, :] & (rank[:, None, :] == ids[:, None])
    lists = jnp.sum(jnp.where(here, ids, 0), axis=2) + jnp.where(ids >= counts[:, None], NB, 0)
    return hot, bias, lists.reshape(-1).astype(jnp.int32), counts


def per_device(query_rows, key_rows, value_rows, out_grad, token_span, visible):
    core = lax.axis_index("core")
    hot, bias, lists, counts = masks(token_span, visible, lax.axis_index("y") * C + core)

    me = lax.axis_index("z")

    def shift(x, axis, size, k):
        return lax.ppermute(x, axis, [(i, (i + k) % size) for i in range(size)])

    def for_head(x, y, c):
        m, n = x.shape[1] // Z, y.shape[1] // Z
        return jnp.concatenate(
            [lax.dynamic_slice_in_dim(x, c * m, m, 1), lax.dynamic_slice_in_dim(y, c * n, n, 1)], axis=1)

    def send(parts, sign):
        return [parts[0]] + [shift(parts[k], "z", Z, sign * k) for k in range(1, Z)]

    def in_order(parts, lo, hi):
        parts = jnp.stack(parts)
        return jnp.concatenate(
            [lax.dynamic_index_in_dim(parts, (c + Z - me) % Z, 0, keepdims=False)[:, lo:hi] for c in range(Z)], axis=1)

    kv = send([for_head(key_rows, value_rows, (me + k) % Z) for k in range(Z)], 1)
    qd = [for_head(query_rows, out_grad, (me + k) % Z) for k in range(Z)]
    kv, qd, hot, bias, lists, counts = lax.optimization_barrier((kv, qd, hot, bias, lists, counts))
    kv = lax.all_gather(jnp.stack(kv), ("y", "core"), axis=0)
    qd = send(qd, 1)
    spot = jnp.stack([core, lax.axis_index("y"), me])
    dq, keep, give = attention(lists, counts, spot, qd, kv, hot, bias)
    dq = send([dq[k] for k in range(Z)], -1)
    other = shift(give, "core", C, 1)
    both = [(keep[k].astype(F32) + other[k].astype(F32)).astype(BF16) for k in range(Y)]
    parts = [both[0]] + [shift(both[k], "y", Y, k) for k in range(1, Y)]
    parts, dq = lax.optimization_barrier((parts, dq))
    dkv = functools.reduce(jnp.add, [part.astype(F32) for part in parts]).astype(BF16)
    dkv = send([dkv[k] for k in range(Z)], -1)
    return in_order(dq, 0, GROUP * HEAD), in_order(dkv, 0, HEAD), in_order(dkv, HEAD, 2 * HEAD)


def solution(mesh):
    dp = mesh.shape["dp"]
    split = Mesh(mesh.devices.reshape(Z, Y, C, dp), ("z", "y", "core", "dp"))
    rows = P(("dp", "z", "y", "core"), None)
    return jax.shard_map(
        per_device,
        mesh=split,
        in_specs=(rows, rows, rows, rows, P("dp"), P("dp", None)),
        out_specs=(rows, rows, rows),
        check_vma=False,
    )
```

```python
import functools

import jax
import jax.numpy as jnp
import numpy as np
from jax import lax
from jax.experimental import pallas as pl
from jax.experimental.pallas import tpu as pltpu
from jax.sharding import Mesh, PartitionSpec as P

HEADS = 12
KV_HEADS = 4
GROUP = HEADS // KV_HEADS
HEAD = 128
SCALE = HEAD ** -0.5
LOG2E = 1.4426950408889634
NEG = -1e30
LIMIT = 48
LEAST = 2.0 ** -60
MOST = 2.0 ** 60
Z, Y, C = 4, 4, 2
T = Y * C
BLK = 192
QT = 256
NQ = Z * BLK // QT
NB = Z * T
WIDE = 8
HALF = WIDE // 2
NI = NB // WIDE
KT = WIDE * BLK
F32 = jnp.float32
BF16 = jnp.bfloat16


def dot(a, b):
    return lax.dot_general(a, b, (((1,), (0,)), ((), ())), preferred_element_type=F32)


def dot_tn(a, b):
    return lax.dot_general(a, b, (((0,), (0,)), ((), ())), preferred_element_type=F32)


def fold(x, op):
    return op(x.reshape(x.shape[0] // 8, 8, x.shape[1]), axis=0)


def attn_kernel(lists, counts, spot, qd0, qd1, qd2, qd3, kv_ref, hot_ref, bias_ref, dq_ref, keep_ref, give_ref,
                qd_all, acc, dpbuf, pbuf, qt, dot_t, qs, dos, stat_m, stat_l, stat_d, stat_c, dqt):
    r = pl.program_id(0)

    def slot(q):
        return (spot[2] + Z - q) % Z

    qd_ref = qd_all.at[pl.ds(pl.multiple_of(r * QT, QT), QT)]

    @pl.when(r == 0)
    def _():
        acc[...] = jnp.zeros_like(acc)
        for k, part in enumerate((qd0, qd1, qd2, qd3)):
            qd_all[pl.ds(pl.multiple_of(slot(k) * BLK, BLK), BLK)] = part[...]

    for h in range(GROUP):
        q = qd_ref[:, h * HEAD:(h + 1) * HEAD]
        g = qd_ref[:, (GROUP + h) * HEAD:(GROUP + h + 1) * HEAD]
        qt[h, :HEAD, :] = q.T
        qt[h, HEAD:, :] = bias_ref[r]
        dot_t[h] = g.T
    dqt[...] = jnp.zeros_like(dqt)
    steps = (counts[r] + HALF - 1) // WIDE
    odd = counts[r] > steps * WIDE

    def blocks(i, wide):
        ids = [lists[r * NB + i * WIDE + j] for j in range(wide)]
        real = [jnp.minimum(b, NB - 1) for b in ids]
        return ids, [(b % T, slot(b // T)) for b in real]

    def masked_keys(ids, where):
        return jnp.concatenate(
            [jnp.concatenate([kv_ref[t, zq, :, :HEAD], hot_ref[b]], axis=1) for b, (t, zq) in zip(ids, where)],
            axis=0)

    def every(body):
        def full(i, carry):
            body(i, WIDE)
            return carry

        lax.fori_loop(0, steps, full, 0)

        @pl.when(odd)
        def _():
            body(steps, HALF)

    def forward(i, wide):
        ids, where = blocks(i, wide)
        lhs = masked_keys(ids, where)
        v = jnp.concatenate([kv_ref[t, zq, :, HEAD:] for t, zq in where], axis=0)
        for h in range(GROUP):
            cols = slice(h * QT, (h + 1) * QT)
            p = jnp.exp2(dot(lhs, qt[h]) * (SCALE * LOG2E))
            dp = dot(v, dot_t[h]) - stat_c[h, :1]
            stat_l[h] += fold(p, jnp.sum)
            stat_d[h] += fold(p * dp, jnp.sum)
            pbuf[i, :wide * BLK, cols] = p.astype(BF16)
            dpbuf[i, :wide * BLK, cols] = dp.astype(BF16)

    _, ((t0, z0),) = blocks(0, 1)
    for h in range(GROUP):
        mean = jnp.sum(dot(kv_ref[t0, z0, :, HEAD:], dot_t[h]), axis=0, keepdims=True) * (1.0 / BLK)
        stat_c[h] = jnp.broadcast_to(mean, (8, QT))

    def forward_all():
        stat_l[...] = jnp.zeros_like(stat_l)
        stat_d[...] = jnp.zeros_like(stat_d)
        every(forward)
        return [jnp.sum(stat_l[h], axis=0, keepdims=True) for h in range(GROUP)]

    sums = forward_all()
    least = jnp.min(functools.reduce(jnp.minimum, sums))
    most = jnp.max(functools.reduce(jnp.maximum, sums))

    @pl.when(jnp.logical_not((least > LEAST) & (most < MOST)))
    def _():
        stat_m[...] = jnp.full_like(stat_m, NEG)

        def tops(i, wide):
            lhs = masked_keys(*blocks(i, wide))
            for h in range(GROUP):
                stat_m[h] = jnp.maximum(stat_m[h], fold(dot(lhs, qt[h]), jnp.max))

        every(tops)
        for h in range(GROUP):
            top = jnp.max(stat_m[h], axis=0, keepdims=True)
            qt[h, HEAD:, :] = (bias_ref[r].astype(F32) - top).astype(BF16)
        forward_all()

    invs = []
    for h in range(GROUP):
        inv = 1.0 / jnp.sum(stat_l[h], axis=0, keepdims=True)
        delta = jnp.sum(stat_d[h], axis=0, keepdims=True) * inv
        stat_d[h] = jnp.broadcast_to(delta, (8, QT))
        col = jnp.broadcast_to(inv, (HEAD, QT)).T
        q = qd_ref[:, h * HEAD:(h + 1) * HEAD].astype(F32)
        g = qd_ref[:, (GROUP + h) * HEAD:(GROUP + h + 1) * HEAD].astype(F32)
        qs[h * QT:(h + 1) * QT] = (q * (col * SCALE)).astype(BF16)
        dos[h * QT:(h + 1) * QT] = (g * col).astype(BF16)
        invs.append(inv)

    def backward(i, wide):
        _, where = blocks(i, wide)
        k = jnp.concatenate([kv_ref[t, zq, :, :HEAD] for t, zq in where], axis=0)
        dv = dot(pbuf[i, :wide * BLK], dos[...])
        dss = []
        for h in range(GROUP):
            cols = slice(h * QT, (h + 1) * QT)
            dss.append((pbuf[i, :wide * BLK, cols].astype(F32) * (dpbuf[i, :wide * BLK, cols].astype(F32) - stat_d[h, :1])).astype(BF16))
        ds = jnp.concatenate(dss, axis=1)
        dqt[...] += dot_tn(k, ds)
        dk = dot(ds, qs[...])
        for j, (t, zq) in enumerate(where):
            acc[t, zq, :, :HEAD] += dk[j * BLK:(j + 1) * BLK]
            acc[t, zq, :, HEAD:] += dv[j * BLK:(j + 1) * BLK]

    every(backward)
    for tile in range(NQ):
        @pl.when(r == tile)
        def _():
            for h in range(GROUP):
                cols = slice(h * QT, (h + 1) * QT)
                dq = (dqt[:, cols] * (invs[h] * SCALE)).T.astype(BF16)
                row = 0
                while row < QT:
                    q, start = divmod(tile * QT + row, BLK)
                    take = min(BLK - start, QT - row)
                    dq_ref[slot(q), start:start + take, h * HEAD:(h + 1) * HEAD] = dq[row:row + take]
                    row += take

    @pl.when(r == NQ - 1)
    def _():
        for i in range(Y):
            y = (spot[1] + i) % Y
            keep_ref[i] = acc[y * C + spot[0]].astype(BF16)
            give_ref[i] = acc[y * C + 1 - spot[0]].astype(BF16)


def attention(lists, counts, spot, qd_parts, kv, hot, bias):
    vmem = pl.BlockSpec(memory_space=pltpu.VMEM)
    return pl.pallas_call(
        attn_kernel,
        grid_spec=pltpu.PrefetchScalarGridSpec(
            num_scalar_prefetch=3,
            grid=(NQ,),
            in_specs=[vmem] * (Z + 3),
            out_specs=[vmem] * 3,
            scratch_shapes=[
                pltpu.VMEM((Z * BLK, 2 * GROUP * HEAD), BF16),
                pltpu.VMEM((T, Z, BLK, 2 * HEAD), F32),
                pltpu.VMEM((NI, KT, GROUP * QT), BF16),
                pltpu.VMEM((NI, KT, GROUP * QT), BF16),
                pltpu.VMEM((GROUP, 2 * HEAD, QT), BF16),
                pltpu.VMEM((GROUP, HEAD, QT), BF16),
                pltpu.VMEM((GROUP * QT, HEAD), BF16),
                pltpu.VMEM((GROUP * QT, HEAD), BF16),
                pltpu.VMEM((GROUP, 8, QT), F32),
                pltpu.VMEM((GROUP, 8, QT), F32),
                pltpu.VMEM((GROUP, 8, QT), F32),
                pltpu.VMEM((GROUP, 8, QT), F32),
                pltpu.VMEM((HEAD, GROUP * QT), F32),
            ],
        ),
        out_shape=[
            jax.ShapeDtypeStruct((Z, BLK, GROUP * HEAD), BF16),
            jax.ShapeDtypeStruct((Y, Z, BLK, 2 * HEAD), BF16),
            jax.ShapeDtypeStruct((Y, Z, BLK, 2 * HEAD), BF16),
        ],
        compiler_params=pltpu.CompilerParams(
            dimension_semantics=("arbitrary",), vmem_limit_bytes=LIMIT * 1024 * 1024
        ),
    )(lists, counts, spot, *qd_parts, kv, hot, bias)


def masks(token_span, visible, t_index):
    spans = token_span.reshape(Z, T, BLK)
    n_spans = visible.shape[0]
    lanes = jnp.arange(HEAD, dtype=jnp.int32)
    empty = jnp.full((1, BLK), n_spans, jnp.int32)
    padded = jnp.concatenate([token_span.reshape(NB, BLK), empty], axis=0)
    hot = (padded[..., None] == lanes).astype(BF16)
    mine = lax.dynamic_index_in_dim(spans, t_index, 1, keepdims=False).reshape(NQ, QT)
    span_ids = jnp.arange(n_spans, dtype=jnp.int32)
    mine_hot = (mine[..., None] == span_ids).astype(F32)
    seen = jnp.einsum("rqs,sk->rkq", mine_hot, visible.astype(F32)) > 0
    bias = jnp.where(seen, 0.0, NEG).astype(BF16)
    bias = jnp.pad(bias, ((0, 0), (0, HEAD - n_spans), (0, 0)), constant_values=NEG)
    key_has = jnp.any(token_span.reshape(NB, BLK)[..., None] == span_ids, axis=1)
    seen_any = jnp.any(seen, axis=2)
    used = jnp.any(key_has[None] & seen_any[:, None], axis=2)
    counts = jnp.sum(used.astype(jnp.int32), axis=1)
    ids = jnp.arange(NB, dtype=jnp.int32)
    rank = jnp.sum((used[:, None, :] & (ids[None, :] <= ids[:, None])).astype(jnp.int32), axis=2) - 1
    here = used[:, None, :] & (rank[:, None, :] == ids[:, None])
    lists = jnp.sum(jnp.where(here, ids, 0), axis=2) + jnp.where(ids >= counts[:, None], NB, 0)
    return hot, bias, lists.reshape(-1).astype(jnp.int32), counts


def per_device(query_rows, key_rows, value_rows, out_grad, token_span, visible):
    core = lax.axis_index("core")
    hot, bias, lists, counts = masks(token_span, visible, lax.axis_index("y") * C + core)

    me = lax.axis_index("z")

    def shift(x, axis, size, k):
        return lax.ppermute(x, axis, [(i, (i + k) % size) for i in range(size)])

    def for_head(x, y, c):
        m, n = x.shape[1] // Z, y.shape[1] // Z
        return jnp.concatenate(
            [lax.dynamic_slice_in_dim(x, c * m, m, 1), lax.dynamic_slice_in_dim(y, c * n, n, 1)], axis=1)

    def send(parts, sign):
        return [parts[0]] + [shift(parts[k], "z", Z, sign * k) for k in range(1, Z)]

    def in_order(parts, lo, hi):
        parts = jnp.stack(parts)
        return jnp.concatenate(
            [lax.dynamic_index_in_dim(parts, (c + Z - me) % Z, 0, keepdims=False)[:, lo:hi] for c in range(Z)], axis=1)

    kv = send([for_head(key_rows, value_rows, (me + k) % Z) for k in range(Z)], 1)
    qd = [for_head(query_rows, out_grad, (me + k) % Z) for k in range(Z)]
    kv, qd, hot, bias, lists, counts = lax.optimization_barrier((kv, qd, hot, bias, lists, counts))
    kv = lax.all_gather(jnp.stack(kv), ("y", "core"), axis=0)
    qd = send(qd, 1)
    spot = jnp.stack([core, lax.axis_index("y"), me])
    dq, keep, give = attention(lists, counts, spot, qd, kv, hot, bias)
    dq = send([dq[k] for k in range(Z)], -1)
    other = shift(give, "core", C, 1)
    both = [(keep[k].astype(F32) + other[k].astype(F32)).astype(BF16) for k in range(Y)]
    parts = [both[0]] + [shift(both[k], "y", Y, k) for k in range(1, Y)]
    parts, dq = lax.optimization_barrier((parts, dq))
    dkv = functools.reduce(jnp.add, [part.astype(F32) for part in parts]).astype(BF16)
    dkv = send([dkv[k] for k in range(Z)], -1)
    return in_order(dq, 0, GROUP * HEAD), in_order(dkv, 0, HEAD), in_order(dkv, HEAD, 2 * HEAD)


def solution(mesh):
    dp = mesh.shape["dp"]
    split = Mesh(mesh.devices.reshape(Z, Y, C, dp), ("z", "y", "core", "dp"))
    rows = P(("dp", "z", "y", "core"), None)
    return jax.shard_map(
        per_device,
        mesh=split,
        in_specs=(rows, rows, rows, rows, P("dp"), P("dp", None)),
        out_specs=(rows, rows, rows),
        check_vma=False,
    )
```
